256 devices in a mesh: dp: 16 (over x, z_hi), pipe: 2 (over z_lo), tensor: 8 (over y, core).
Axes of the slice: x: 4, y: 4, z: 8 (z_hi: 4, z_lo: 2; z = z_hi * 2 + z_lo), core: 2. Of those that a mesh axis runs over, the one named last changes fastest.
Arguments:
- sent_qkv: bfloat16 [2, 16, 384, 3, 6144], P('pipe', 'dp', None, None, 'tensor'), may hold values from -64 to 64
- saved_qkv: bfloat16 [2, 16, 384, 3, 6144], P('pipe', 'dp', None, None, 'tensor'), may hold values from -64 to 64
- cotangent: bfloat16 [2, 16, 384, 6144], P('pipe', 'dp', None, 'tensor'), may hold values from -6 to 6
- out_weight: bfloat16 [2, 6144, 6144], P('pipe', 'tensor', 'dp'), may hold values from -0.078125 to 0.078125
Outputs:
- section_out: bfloat16 [2, 16, 384, 6144], P('pipe', 'dp', None, 'tensor')
- qkv_grad: bfloat16 [2, 16, 384, 3, 6144], P('pipe', 'dp', None, None, 'tensor')
- weight_grad: bfloat16 [2, 6144, 6144], P('pipe', 'tensor', 'dp')
The draws below stay inside these ranges and needn't reach their ends.
All inputs are finite; a program needn't handle non-finite values.
Results may differ from the reference program's by a relative error of at most 0.019.
Values may be sent and summed in bfloat16 or wider, within the bound.
A program may use at most 128 MiB of HBM per device.

```python
import math
import jax
import jax.numpy as jnp
from jax import lax

D = 6144
HEADS = 48
HEAD_DIM = 128
SEQ = 384
HW = 6144
N_DP = 16
N_PIPE = 2
N_TENSOR = 8


def clipped_normal(key):
    shape = (N_PIPE, N_DP, SEQ, 3, HEADS * HEAD_DIM)
    return jnp.clip(jax.random.normal(key, shape, jnp.float32), -4.0, 4.0)


def draw_sent_qkv(key, part):
    key = jax.random.fold_in(key, 5)
    values = clipped_normal(key)
    return values.astype(jnp.bfloat16)


def draw_saved_qkv(key, part):
    key = jax.random.fold_in(key, 7)
    values = clipped_normal(key)
    return values.astype(jnp.bfloat16)


def with_spikes(drawn, rng, source, target, shards_of, factor):
    def block_of(dim):
        return (jnp.arange(drawn.shape[dim]) // (drawn.shape[dim] // shards_of)).reshape((-1,) + (1,) * (drawn.ndim - 1 - dim))

    first = jax.random.permutation(rng, shards_of)[block_of(target)]
    other_side = (block_of(target) + shards_of // 2) % shards_of
    return jnp.where((block_of(source) == first) | (block_of(source) == other_side), factor * drawn, drawn)


def levels(own_key, shape, split, low, top_value):
    loudness, own = 1.0, jax.random.fold_in(own_key, 6)
    for axis_at, shards_of in split:
        heights = jnp.exp(jax.random.uniform(jax.random.fold_in(own, axis_at), (shards_of,), jnp.float32, low / len(split), top_value / len(split)))
        loudness = loudness * jnp.repeat(heights, shape[axis_at] // shards_of).reshape([-1 if axis == axis_at else 1 for axis in range(len(shape))])
    return loudness


def bell_draw(stream_key, shape, spread, bound, cuts=(), dtype=jnp.bfloat16):
    drawn = jax.random.normal(stream_key, shape, jnp.float32) * spread
    if len(cuts) > 0:
        drawn = levels(stream_key, shape, cuts, -0.22, 0.18) * drawn
    return jnp.clip(drawn, min=-bound, max=bound).astype(dtype)


def noise_with(stream_key, dims, deviation, bound, cuts, heavy, dtype=jnp.bfloat16):
    result = deviation * jax.random.normal(stream_key, dims, jnp.float32)
    if cuts:
        result = result * levels(stream_key, dims, cuts, -0.22, 0.18)
    return jnp.clip(with_spikes(result, jax.random.fold_in(stream_key, 3), *heavy), -bound, bound).astype(dtype)


def setup_inputs(seed: int = 0) -> dict:
    streams_of = jax.random.split(jax.random.key(seed), 5)
    sent_qkv = draw_sent_qkv(jax.random.fold_in(streams_of[4], 71), 0)
    saved_qkv = draw_saved_qkv(jax.random.fold_in(streams_of[4], 71), 0)
    cotangent = noise_with(streams_of[2], (N_PIPE, N_DP, SEQ, D), 1.0, 6.0, ((0, 2), (1, 16), (3, 8)), (1, 3, 16, 2.0))
    out_weight = bell_draw(streams_of[3], (N_PIPE, HW, D), HW ** -0.5, 0.078125, ((0, 2), (1, 8), (2, 16)))
    return {"sent_qkv": sent_qkv, "saved_qkv": saved_qkv, "cotangent": cotangent, "out_weight": out_weight}


def settle(values):
    return lax.optimization_barrier(values.astype(jnp.bfloat16)).astype(jnp.float32)

def heads_forward(triple):
    pieces = triple.astype(jnp.float32).reshape(SEQ, 3, HEADS, HEAD_DIM)
    scores = jnp.einsum('ihd,jhd->hij', pieces[:, 0], pieces[:, 1]) / math.sqrt(HEAD_DIM)
    causal = jnp.arange(SEQ)[:, None] >= jnp.arange(SEQ)[None, :]
    scores = jnp.where(causal[None], scores, -jnp.inf)
    attention_w = jax.nn.softmax(scores, axis=-1)
    attention_b = settle(attention_w)
    context = jnp.einsum('hij,jhd->ihd', attention_b, pieces[:, 2]).reshape(SEQ, HEADS * HEAD_DIM)
    return (attention_w, attention_b, settle(context))

def heads_backward(triple, attention_w, attention_b, context_grad):
    pieces = triple.astype(jnp.float32).reshape(SEQ, 3, HEADS, HEAD_DIM)
    upstream = context_grad.reshape(SEQ, HEADS, HEAD_DIM)
    attention_dw = jnp.einsum('ihd,jhd->hij', upstream, pieces[:, 2])
    row_total = lax.optimization_barrier(jnp.sum(attention_w * attention_dw, axis=-1, keepdims=True))
    score_grad = settle(attention_w * (attention_dw - row_total) / math.sqrt(HEAD_DIM))
    query_grad = jnp.einsum('hij,jhd->ihd', score_grad, pieces[:, 1])
    key_grad = jnp.einsum('hij,ihd->jhd', score_grad, pieces[:, 0])
    value_grad = jnp.einsum('hij,ihd->jhd', attention_b, upstream)
    stacked = jnp.stack([query_grad, key_grad, value_grad], axis=1)
    return stacked.reshape(SEQ, 3, HEADS * HEAD_DIM).astype(jnp.bfloat16)

def reference(sent_qkv, saved_qkv, cotangent, out_weight):
    width = HEADS * HEAD_DIM
    group = width // N_TENSOR
    section_list = []
    grad_list = []
    weight_list = []
    for section in range(N_PIPE):
        weight = out_weight[section]
        weight_groups = weight.astype(jnp.float32).reshape(N_TENSOR, group, D)

        def forward_one(triple):
            context = heads_forward(triple)[2]
            partial_out = jnp.einsum('sgk,gkd->gsd', context.reshape(SEQ, N_TENSOR, group), weight_groups)
            return lax.optimization_barrier(jnp.sum(settle(partial_out), axis=0)).astype(jnp.bfloat16)
        section_list.append(lax.map(forward_one, sent_qkv[(section - 1) % N_PIPE]))

        def backward_one(total, inputs):
            triple, upstream = inputs
            attention_w, attention_b, context = heads_forward(triple)
            context_grad = settle(jnp.dot(upstream, weight.T, preferred_element_type=jnp.float32))
            grad_triple = heads_backward(triple, attention_w, attention_b, context_grad)
            partial_grad = settle(jnp.dot(context.T, upstream.astype(jnp.float32)))
            return (total + partial_grad, grad_triple)
        total, grad_triple = lax.scan(backward_one, jnp.zeros((width, D), jnp.float32), (saved_qkv[section], cotangent[section]))
        grad_list.append(grad_triple)
        weight_list.append((total / N_DP).astype(jnp.bfloat16))
    return (jnp.stack(section_list), jnp.stack(grad_list), jnp.stack(weight_list))
```

```python
import math

import jax
import jax.numpy as jnp
from jax import lax
from jax.experimental import pallas as pl
from jax.experimental.pallas import tpu as pltpu
from jax.sharding import PartitionSpec as P

HEAD_DIM = 128
SCALE = 1.0 / math.sqrt(HEAD_DIM)
MESH = pl.DeviceIdType.MESH
BF = jnp.bfloat16
F32 = jnp.float32
S = 384
W = 768
HEADS = W // HEAD_DIM
N_SEMS = 64

NT = (((1,), (1,)), ((), ()))
TN = (((0,), (0,)), ((), ()))


def at(index, size):
    return pl.ds(pl.multiple_of(index * size, size), size)


def mod4(i):
    return lax.rem(i + 4, 4)


def attend(qkv, h):
    cols = at(h, HEAD_DIM)
    scores = lax.dot_general(qkv[0, :, cols], qkv[1, :, cols], NT, preferred_element_type=F32)
    row = lax.broadcasted_iota(jnp.int32, (S, S), 0)
    col = lax.broadcasted_iota(jnp.int32, (S, S), 1)
    scores = jnp.where(row >= col, scores * SCALE, -jnp.inf)
    weights = jnp.exp(scores - jnp.max(scores, axis=1, keepdims=True))
    probs = weights / jnp.sum(weights, axis=1, keepdims=True)
    return jnp.dot(probs.astype(BF), qkv[2, :, cols], preferred_element_type=F32).astype(BF)


def attend_t(qkv, h, probs_t):
    cols = at(h, HEAD_DIM)
    scores = lax.dot_general(qkv[1, :, cols], qkv[0, :, cols], NT, preferred_element_type=F32)
    row = lax.broadcasted_iota(jnp.int32, (S, S), 0)
    col = lax.broadcasted_iota(jnp.int32, (S, S), 1)
    scores = jnp.where(row <= col, scores * SCALE, -jnp.inf)
    weights = jnp.exp(scores - jnp.max(scores, axis=0, keepdims=True))
    probs = weights / jnp.sum(weights, axis=0, keepdims=True)
    probs_t[h] = probs
    return lax.dot_general(
        qkv[2, :, cols], probs.astype(BF), TN, preferred_element_type=F32
    ).astype(BF)


def attend_grad(qkv, h, probs_t, upstream, grads):
    cols = at(h, HEAD_DIM)
    probs = probs_t[h]
    up = upstream[:, cols]
    d_probs = lax.dot_general(qkv[2, :, cols], up, NT, preferred_element_type=F32)
    total = jnp.sum(probs * d_probs, axis=0, keepdims=True)
    d_scores = (probs * (d_probs - total) * SCALE).astype(BF)
    dq_t = lax.dot_general(qkv[1, :, cols], d_scores, TN, preferred_element_type=F32)
    grads[0, :, cols] = dq_t.T.astype(BF)
    grads[1, :, cols] = jnp.dot(d_scores, qkv[0, :, cols], preferred_element_type=F32).astype(BF)
    grads[2, :, cols] = jnp.dot(probs.astype(BF), up, preferred_element_type=F32).astype(BF)


class Ring:
    def __init__(self, remote, me, plus, minus):
        self.remote, self.me, self.plus, self.minus = remote, me, plus, minus

    def gather_half(self, block, h, source=None):
        src = block(self.me, h) if source is None else source
        dst = block(self.me, h)
        to_plus = self.remote(src, dst, self.plus)
        to_minus = self.remote(src, dst, self.minus)
        first, second = (to_plus, to_minus) if h == 0 else (to_minus, to_plus)
        first.start()
        second.start()
        if h == 0:
            self.plus0, self.minus0 = to_plus, to_minus
        else:
            self.plus1, self.minus1 = to_plus, to_minus

    def gather_forward(self, block):
        prev, nxt = mod4(self.me - 1), mod4(self.me + 1)
        self.plus0.wait_recv()
        self.far0 = self.remote(block(prev, 0), block(prev, 0), self.plus)
        self.far0.start()
        self.minus1.wait_recv()
        self.far1 = self.remote(block(nxt, 1), block(nxt, 1), self.minus)
        self.far1.start()

    def gather_near(self):
        self.plus1.wait_recv()
        self.minus0.wait_recv()

    def gather_far(self):
        self.far0.wait_recv()
        self.far1.wait_recv()

    def reduce_far(self, part, got_far):
        far = mod4(self.me + 2)
        self.r0 = self.remote(part(far, 0), got_far.at[0], self.plus)
        self.r1 = self.remote(part(far, 1), got_far.at[1], self.minus)
        self.r0.start()
        self.r1.start()

    def reduce_near(self, part, got_near):
        nxt, prev = mod4(self.me + 1), mod4(self.me - 1)
        self.r2 = self.remote(part(nxt, 1), got_near.at[0, 1], self.plus)
        self.r3 = self.remote(part(prev, 0), got_near.at[1, 0], self.minus)
        self.r2.start()
        self.r3.start()

    def reduce_pass(self, part, got_far, got_near):
        nxt, prev = mod4(self.me + 1), mod4(self.me - 1)
        self.r0.wait_recv()
        ref = part(nxt, 0)
        ref[...] = (ref[...].astype(F32) + got_far[0].astype(F32)).astype(BF)
        self.r4 = self.remote(ref, got_near.at[0, 0], self.plus)
        self.r4.start()
        self.r1.wait_recv()
        ref = part(prev, 1)
        ref[...] = (ref[...].astype(F32) + got_far[1].astype(F32)).astype(BF)
        self.r5 = self.remote(ref, got_near.at[1, 1], self.minus)
        self.r5.start()

    def reduce_sum(self, part, got_near, h):
        for copy in ((self.r4, self.r3), (self.r2, self.r5))[h]:
            copy.wait_recv()
        total = part(self.me, h)[...].astype(F32)
        return total + got_near[0, h].astype(F32) + got_near[1, h].astype(F32)


def kernel(
    qkv_a_hbm, qkv_b_hbm, cot_hbm, w_hbm,
    out_ref, grads_ref, w_grad_ref,
    qkv_a, qkv_b, w_all, cot_all, ctx_a, ctx_a_all, ctx_b_all, probs_t,
    w_part, w_far, w_near, c_part, c_far, c_near, c_grad,
    o_own, o_other, o_got, o_far, o_near, o_done,
    send_sems, recv_sems, local_sems,
):
    dp, pipe, tensor = lax.axis_index("dp"), lax.axis_index("pipe"), lax.axis_index("tensor")
    x, z, y, core = dp // 4, lax.rem(dp, 4), tensor // 2, lax.rem(tensor, 2)

    def device(x=x, z=z, pipe=pipe, y=y, core=core):
        return (x * 4 + z, pipe, y * 2 + core)

    x_plus, x_minus = device(x=mod4(x + 1)), device(x=mod4(x - 1))
    y_plus, y_minus = device(y=mod4(y + 1)), device(y=mod4(y - 1))
    z_plus, z_minus = device(z=mod4(z + 1)), device(z=mod4(z - 1))
    twin, other_pipe, mirror = device(core=1 - core), device(pipe=1 - pipe), device(x=y, y=x)
    off_diagonal = x != y

    barrier = pltpu.get_barrier_semaphore()
    for partner in (x_plus, x_minus, y_plus, y_minus, z_plus, z_minus, twin, other_pipe):
        pl.semaphore_signal(barrier, inc=1, device_id=partner, device_id_type=MESH)

    @pl.when(off_diagonal)
    def _():
        pl.semaphore_signal(barrier, inc=1, device_id=mirror, device_id_type=MESH)

    pl.semaphore_wait(barrier, jnp.where(off_diagonal, 9, 8))

    made = []

    def remote(src, dst, where):
        copy = pltpu.make_async_remote_copy(
            src_ref=src, dst_ref=dst,
            send_sem=send_sems.at[len(made)], recv_sem=recv_sems.at[len(made)],
            device_id=where, device_id_type=MESH,
        )
        made.append(copy)
        return copy

    def w_block(i, h):
        return w_all.at[pl.ds(h * S, S), at(i, S)]

    def cot_block(i, h):
        return cot_all.at[at(2 * i + h, S // 2), at(core, W)]

    def ctx_a_block(i, h):
        return ctx_a_all.at[at(i, S), pl.ds(h * S, S)]

    def ctx_b_block(i, h):
        return ctx_b_all.at[pl.ds(h * S, S), at(i, S)]

    def w_part_block(i, h):
        return w_part.at[i, h]

    def c_part_block(i, h):
        return c_part.at[i, h]

    def o_block(i, h):
        return o_own.at[i, h]

    ring_w = Ring(remote, z, z_plus, z_minus)
    ring_cot = Ring(remote, y, y_plus, y_minus)
    ring_a = Ring(remote, x, x_plus, x_minus)
    ring_b = Ring(remote, x, x_plus, x_minus)
    ring_wg = Ring(remote, z, z_plus, z_minus)
    ring_cg = Ring(remote, x, x_plus, x_minus)
    ring_out = Ring(remote, y, y_plus, y_minus)

    for h in (0, 1):
        ring_w.gather_half(w_block, h, w_hbm.at[pl.ds(h * S, S)])
    cot_mine = cot_all.at[at(y, S), at(core, W)]
    cot_there = cot_all.at[at(x, S), at(core, W)]
    mirrored = remote(cot_hbm, cot_there, mirror)
    cot_local = pltpu.make_async_copy(cot_hbm, cot_mine, local_sems.at[0])

    @pl.when(off_diagonal)
    def _():
        mirrored.start()

    @pl.when(jnp.logical_not(off_diagonal))
    def _():
        cot_local.start()

    load_a = pltpu.make_async_copy(qkv_a_hbm, qkv_a, local_sems.at[1])
    load_b = pltpu.make_async_copy(qkv_b_hbm, qkv_b, local_sems.at[2])
    load_w = pltpu.make_async_copy(w_hbm, w_all.at[:, at(z, S)], local_sems.at[3])
    load_a.start()
    load_b.start()
    load_w.start()

    handed = []
    load_a.wait()
    for h in (0, 1):
        def head_a(i, carry, h=h):
            head = h * (HEADS // 2) + i
            ctx_a[:, at(head, HEAD_DIM)] = attend(qkv_a, head)
            return carry
        lax.fori_loop(0, HEADS // 2, head_a, 0)
        copy = remote(ctx_a.at[:, pl.ds(h * S, S)], ctx_a_block(x, h), other_pipe)
        copy.start()
        handed.append(copy)

    load_b.wait()
    for h in (0, 1):
        def head_b(i, carry, h=h):
            head = h * (HEADS // 2) + i
            ctx_b_all[at(head, HEAD_DIM), at(x, S)] = attend_t(qkv_b, head, probs_t)
            return carry
        lax.fori_loop(0, HEADS // 2, head_b, 0)
        ring_b.gather_half(ctx_b_block, h)

    @pl.when(off_diagonal)
    def _():
        mirrored.wait_recv()

    @pl.when(jnp.logical_not(off_diagonal))
    def _():
        cot_local.wait()

    def to_twin(i):
        ref = cot_all.at[at(i, S), at(core, W)]
        copy = remote(ref, ref, twin)
        copy.start()
        return copy

    for h in (0, 1):
        ring_cot.gather_half(cot_block, h)
    twins = [to_twin(y)]
    ring_b.gather_forward(ctx_b_block)
    for h in (0, 1):
        handed[h].wait_recv()
        ring_a.gather_half(ctx_a_block, h)
    ring_cot.gather_forward(cot_block)
    ring_w.gather_forward(w_block)
    ring_cot.gather_near()
    twins += [to_twin(mod4(y - 1)), to_twin(mod4(y + 1))]
    ring_a.gather_forward(ctx_a_block)
    ring_cot.gather_far()
    twins += [to_twin(mod4(y + 2))]
    ring_b.gather_near()
    ring_b.gather_far()
    for copy in twins:
        copy.wait_recv()

    def w_term(i):
        def rows(r, carry):
            w_part[i, r] = jnp.dot(
                ctx_b_all[at(r, S), :], cot_all[:, at(i, S)], preferred_element_type=F32
            ).astype(BF)
            return carry
        lax.fori_loop(0, 2, rows, 0)

    w_term(mod4(z + 2))
    ring_wg.reduce_far(w_part_block, w_far)
    w_term(mod4(z + 1))
    w_term(mod4(z - 1))
    ring_wg.reduce_near(w_part_block, w_near)
    w_term(z)

    load_w.wait()
    ring_w.gather_near()
    ring_w.gather_far()

    def c_term(i):
        def rows(r, carry):
            c_part[i, r] = lax.dot_general(
                cot_all[at(2 * i + r, S // 2), :], w_all[...], NT, preferred_element_type=F32
            ).astype(BF)
            return carry
        lax.fori_loop(0, 2, rows, 0)

    c_term(mod4(x + 2))
    ring_cg.reduce_far(c_part_block, c_far)
    c_term(mod4(x + 1))
    c_term(mod4(x - 1))
    ring_cg.reduce_near(c_part_block, c_near)
    c_term(x)

    ring_a.gather_near()
    ring_a.gather_far()

    def o_term(i, r, side):
        return jnp.dot(
            ctx_a_all[at(2 * i + r, S // 2), :], w_all[:, at(side, W)], preferred_element_type=F32
        )

    def o_other_rows(j, carry):
        o_other[j // 2, lax.rem(j, 2)] = o_term(j // 2, lax.rem(j, 2), 1 - core).astype(BF)
        return carry

    lax.fori_loop(0, 8, o_other_rows, 0)
    swap = remote(o_other, o_got, twin)
    swap.start()
    ring_wg.reduce_pass(w_part_block, w_far, w_near)
    ring_cg.reduce_pass(c_part_block, c_far, c_near)
    swap.wait_recv()

    def o_sum(i):
        def rows(r, carry):
            o_own[i, r] = (o_term(i, r, core) + o_got[i, r].astype(F32)).astype(BF)
            return carry
        lax.fori_loop(0, 2, rows, 0)

    o_sum(mod4(y + 2))
    ring_out.reduce_far(o_block, o_far)
    o_sum(mod4(y + 1))
    o_sum(mod4(y - 1))
    ring_out.reduce_near(o_block, o_near)
    o_sum(y)

    for h in (0, 1):
        c_grad[pl.ds(h * (S // 2), S // 2)] = ring_cg.reduce_sum(c_part_block, c_near, h).astype(BF)
    ring_out.reduce_pass(o_block, o_far, o_near)

    def head_grad(h, carry):
        attend_grad(qkv_b, h, probs_t, c_grad, grads_ref)
        return carry

    lax.fori_loop(0, HEADS, head_grad, 0)

    for h in (0, 1):
        o_done[pl.ds(h * (S // 2), S // 2)] = ring_out.reduce_sum(o_block, o_near, h).astype(BF)
    back = remote(o_done, out_ref, mirror)

    @pl.when(off_diagonal)
    def _():
        back.start()

    @pl.when(jnp.logical_not(off_diagonal))
    def _():
        out_ref[...] = o_done[...]

    for h in (0, 1):
        w_grad_ref[pl.ds(h * S, S)] = (
            ring_wg.reduce_sum(w_part_block, w_near, h) / lax.axis_size("dp")
        ).astype(BF)

    @pl.when(off_diagonal)
    def _():
        back.wait_recv()

    for copy in made:
        if copy is mirrored or copy is back:
            continue
        copy.wait_send()

    @pl.when(off_diagonal)
    def _():
        mirrored.wait_send()
        back.wait_send()


def body(sent_qkv, saved_qkv, cotangent, out_weight):
    bf = lambda *shape: pltpu.VMEM(shape, BF)
    half = S // 2
    out, grads, w_grad = pl.pallas_call(
        kernel,
        out_shape=(
            jax.ShapeDtypeStruct((S, W), BF),
            jax.ShapeDtypeStruct((3, S, W), BF),
            jax.ShapeDtypeStruct((W, S), BF),
        ),
        in_specs=[pl.BlockSpec(memory_space=pl.ANY)] * 4,
        out_specs=(pl.BlockSpec(memory_space=pltpu.VMEM),) * 3,
        scratch_shapes=[
            bf(3, S, W), bf(3, S, W),
            bf(W, 4 * S), bf(4 * S, 2 * W),
            bf(S, W), bf(4 * S, W), bf(W, 4 * S),
            pltpu.VMEM((HEADS, S, S), F32),
            bf(4, 2, S, S), bf(2, S, S), bf(2, 2, S, S),
            bf(4, 2, half, W), bf(2, half, W), bf(2, 2, half, W), bf(S, W),
            bf(4, 2, half, W), bf(4, 2, half, W), bf(4, 2, half, W),
            bf(2, half, W), bf(2, 2, half, W), bf(S, W),
            pltpu.SemaphoreType.DMA((N_SEMS,)),
            pltpu.SemaphoreType.DMA((N_SEMS,)),
            pltpu.SemaphoreType.DMA((4,)),
        ],
        compiler_params=pltpu.CompilerParams(
            collective_id=0, has_side_effects=True, vmem_limit_bytes=56 << 20
        ),
        cost_estimate=pl.CostEstimate(
            flops=13_000_000_000, bytes_accessed=16_000_000, transcendentals=1_800_000
        ),
    )(
        jnp.transpose(sent_qkv[0, 0], (1, 0, 2)),
        jnp.transpose(saved_qkv[0, 0], (1, 0, 2)),
        cotangent[0, 0],
        out_weight[0],
    )
    return out[None, None], jnp.transpose(grads, (1, 0, 2))[None, None], w_grad[None]


def solution(mesh):
    in_specs = (
        P("pipe", "dp", None, None, "tensor"),
        P("pipe", "dp", None, None, "tensor"),
        P("pipe", "dp", None, "tensor"),
        P("pipe", "tensor", "dp"),
    )
    out_specs = (
        P("pipe", "dp", None, "tensor"),
        P("pipe", "dp", None, None, "tensor"),
        P("pipe", "tensor", "dp"),
    )
    return jax.shard_map(body, mesh=mesh, in_specs=in_specs, out_specs=out_specs, check_vma=False)
```

```python
import math

import jax
import jax.numpy as jnp
from jax import lax
from jax.experimental import pallas as pl
from jax.experimental.pallas import tpu as pltpu
from jax.sharding import PartitionSpec as P

HEAD_DIM = 128
SCALE = 1.0 / math.sqrt(HEAD_DIM)
MESH = pl.DeviceIdType.MESH
BF = jnp.bfloat16
F32 = jnp.float32
S = 384
W = 768
HEADS = W // HEAD_DIM
N_SEMS = 96
PIECES = S // HEAD_DIM

NT = (((1,), (1,)), ((), ()))
TN = (((0,), (0,)), ((), ()))


def at(index, size):
    return pl.ds(pl.multiple_of(index * size, size), size)


def mod4(i):
    return lax.rem(i + 4, 4)


def causal_blocks():
    for r in range(S // HEAD_DIM):
        yield r, pl.ds(r * HEAD_DIM, HEAD_DIM), pl.ds(0, (r + 1) * HEAD_DIM)


def probs_of_block(qkv, cols, r, mine, seen):
    scores = lax.dot_general(qkv[1, seen, cols], qkv[0, mine, cols], NT, preferred_element_type=F32)
    row = lax.broadcasted_iota(jnp.int32, scores.shape, 0)
    col = lax.broadcasted_iota(jnp.int32, scores.shape, 1) + r * HEAD_DIM
    scores = jnp.where(row <= col, scores, -jnp.inf)
    weights = jnp.exp((scores - jnp.max(scores, axis=0, keepdims=True)) * SCALE)
    return weights * (1.0 / jnp.sum(weights, axis=0, keepdims=True))


def attend(qkv, h, block, context):
    cols = at(h, HEAD_DIM)
    r, mine, seen = block
    probs = probs_of_block(qkv, cols, r, mine, seen).astype(BF)
    context_t = lax.dot_general(qkv[2, seen, cols], probs, TN, preferred_element_type=F32)
    context[mine, cols] = context_t.T.astype(BF)


def attend_t(qkv, h, context_t, probs_t, x):
    cols = at(h, HEAD_DIM)
    for r, mine, seen in causal_blocks():
        probs = probs_of_block(qkv, cols, r, mine, seen)
        probs_t[h, seen, mine] = probs
        context_t[cols, at(x * (S // HEAD_DIM) + r, HEAD_DIM)] = lax.dot_general(
            qkv[2, seen, cols], probs.astype(BF), TN, preferred_element_type=F32
        ).astype(BF)


def attend_grad(qkv, h, probs_t, upstream, grads):
    cols = at(h, HEAD_DIM)
    dk, dv = [0.0] * 3, [0.0] * 3
    for r, mine, seen in causal_blocks():
        probs = probs_t[h, seen, mine]
        up = upstream[mine, cols]
        d_probs = lax.dot_general(qkv[2, seen, cols], up, NT, preferred_element_type=F32)
        total = jnp.sum(probs * d_probs, axis=0, keepdims=True)
        d_scores = (probs * (d_probs - total) * SCALE).astype(BF)
        dq_t = lax.dot_general(qkv[1, seen, cols], d_scores, TN, preferred_element_type=F32)
        grads[0, mine, cols] = dq_t.T.astype(BF)
        dk_r = jnp.dot(d_scores, qkv[0, mine, cols], preferred_element_type=F32)
        dv_r = jnp.dot(probs.astype(BF), up, preferred_element_type=F32)
        for j in range(r + 1):
            rows = slice(j * HEAD_DIM, (j + 1) * HEAD_DIM)
            dk[j] += dk_r[rows]
            dv[j] += dv_r[rows]
    for j in range(3):
        rows = pl.ds(j * HEAD_DIM, HEAD_DIM)
        grads[1, rows, cols] = dk[j].astype(BF)
        grads[2, rows, cols] = dv[j].astype(BF)


class Ring:
    def __init__(self, remote, me, plus, minus):
        self.remote, self.me, self.plus, self.minus = remote, me, plus, minus

    def gather_first(self, block, h, source=None):
        dst = block(self.me, h)
        copy = self.remote(dst if source is None else source, dst, (self.plus, self.minus)[h])
        copy.start()
        if h == 0:
            self.plus0 = copy
        else:
            self.minus1 = copy

    def gather_second(self, block, h, source=None):
        dst = block(self.me, h)
        copy = self.remote(dst if source is None else source, dst, (self.minus, self.plus)[h])
        copy.start()
        if h == 0:
            self.minus0 = copy
        else:
            self.plus1 = copy

    def gather_forward(self, block):
        prev, nxt = mod4(self.me - 1), mod4(self.me + 1)
        self.plus0.wait_recv()
        self.far0 = self.remote(block(prev, 0), block(prev, 0), self.plus)
        self.far0.start()
        self.minus1.wait_recv()
        self.far1 = self.remote(block(nxt, 1), block(nxt, 1), self.minus)
        self.far1.start()

    def gather_near(self):
        self.plus1.wait_recv()
        self.minus0.wait_recv()

    def gather_far(self):
        self.far0.wait_recv()
        self.far1.wait_recv()

    def reduce_far(self, part, got_far):
        far = mod4(self.me + 2)
        self.r0 = self.remote(part(far, 0), got_far.at[0], self.plus)
        self.r1 = self.remote(part(far, 1), got_far.at[1], self.minus)
        self.r0.start()
        self.r1.start()

    def reduce_near(self, part, got_near):
        nxt, prev = mod4(self.me + 1), mod4(self.me - 1)
        self.r2 = self.remote(part(nxt, 1), got_near.at[0, 1], self.plus)
        self.r3 = self.remote(part(prev, 0), got_near.at[1, 0], self.minus)
        self.r2.start()
        self.r3.start()

    def reduce_pass(self, part, got_far, got_near):
        nxt, prev = mod4(self.me + 1), mod4(self.me - 1)
        self.r0.wait_recv()
        ref = part(nxt, 0)
        ref[...] = (ref[...].astype(F32) + got_far[0].astype(F32)).astype(BF)
        self.r4 = self.remote(ref, got_near.at[0, 0], self.plus)
        self.r4.start()
        self.r1.wait_recv()
        ref = part(prev, 1)
        ref[...] = (ref[...].astype(F32) + got_far[1].astype(F32)).astype(BF)
        self.r5 = self.remote(ref, got_near.at[1, 1], self.minus)
        self.r5.start()

    def reduce_sum(self, part, got_near, h):
        for copy in ((self.r4, self.r3), (self.r2, self.r5))[h]:
            copy.wait_recv()
        total = part(self.me, h)[...].astype(F32)
        return total + got_near[0, h].astype(F32) + got_near[1, h].astype(F32)


def kernel(
    qkv_a_hbm, qkv_b_hbm, cot_hbm, w_hbm,
    out_ref, grads_ref, w_grad_ref,
    qkv_a, qkv_b, w_all, cot_all, cot_relay, ctx_a, ctx_a_all, ctx_b_all, probs_t,
    w_part, w_far, w_near, c_part, c_far, c_near, c_grad,
    o_own, o_other, o_got, o_far, o_near, o_done,
    send_sems, recv_sems, local_sems,
):
    dp, pipe, tensor = lax.axis_index("dp"), lax.axis_index("pipe"), lax.axis_index("tensor")
    x, z, y, core = dp // 4, lax.rem(dp, 4), tensor // 2, lax.rem(tensor, 2)

    def device(x=x, z=z, pipe=pipe, y=y, core=core):
        return (x * 4 + z, pipe, y * 2 + core)

    x_plus, x_minus = device(x=mod4(x + 1)), device(x=mod4(x - 1))
    y_plus, y_minus = device(y=mod4(y + 1)), device(y=mod4(y - 1))
    z_plus, z_minus = device(z=mod4(z + 1)), device(z=mod4(z - 1))
    twin, other_pipe = device(core=1 - core), device(pipe=1 - pipe)

    there = mod4(y - x + 2 * core)
    down, across = device(y=mod4(x + y + 2 * core)), device(x=there)
    home, away = device(x=there, y=x), device(x=y, y=mod4(x + y + 2 * core))
    stays_down, stays_across = lax.rem(x + 2 * core, 4) == 0, there == x
    stays_home = jnp.logical_and(there == x, y == x)

    barrier = pltpu.get_barrier_semaphore()
    for partner in (
        x_plus, x_minus, device(x=mod4(x + 2)), y_plus, y_minus, device(y=mod4(y + 2)),
        z_plus, z_minus, twin, other_pipe,
    ):
        pl.semaphore_signal(barrier, inc=1, device_id=partner, device_id_type=MESH)

    @pl.when(jnp.logical_not(stays_home))
    def _():
        for partner in (home, away):
            pl.semaphore_signal(barrier, inc=1, device_id=partner, device_id_type=MESH)

    pl.semaphore_wait(barrier, jnp.where(stays_home, 10, 12))

    made = []

    def remote(src, dst, where):
        copy = pltpu.make_async_remote_copy(
            src_ref=src, dst_ref=dst,
            send_sem=send_sems.at[len(made)], recv_sem=recv_sems.at[len(made)],
            device_id=where, device_id_type=MESH,
        )
        made.append(copy)
        return copy

    class Move:
        def __init__(self, src, dst_there, dst_here, where, stays, local_sem):
            self.stays, self.copy = stays, remote(src, dst_there, where)
            self.local = pltpu.make_async_copy(src, dst_here, local_sem)

        def start(self):
            pl.when(self.stays)(lambda: self.local.start())
            pl.when(jnp.logical_not(self.stays))(lambda: self.copy.start())

        def wait_recv(self):
            pl.when(self.stays)(lambda: self.local.wait())
            pl.when(jnp.logical_not(self.stays))(lambda: self.copy.wait_recv())

        def wait_send(self):
            pl.when(jnp.logical_not(self.stays))(lambda: self.copy.wait_send())

    moves = []

    def move(*args):
        moves.append(Move(*args))
        moves[-1].start()
        return moves[-1]

    def place_tokens(i):
        return mod4(i - x + 2 * core)

    def w_block(i, h):
        return w_all.at[pl.ds(h * S, S), at(i, S)]

    def cot_block(i, h):
        return cot_all.at[at(2 * place_tokens(i) + h, S // 2), at(core, W)]

    def a_rows(p, i):
        return at(p * 4 + i, HEAD_DIM)

    def ctx_a_block(p):
        return lambda i, h: ctx_a_all.at[a_rows(p, i), pl.ds(h * S, S)]

    def ctx_b_block(i, h):
        return ctx_b_all.at[pl.ds(h * S, S), at(i, S)]

    def w_part_block(i, h):
        return w_part.at[i, h]

    def c_part_block(i, h):
        return c_part.at[i, h]

    def o_block(p):
        return lambda i, h: o_own.at[a_rows(p, place_tokens(i)), pl.ds(h * S, S)]

    ring_w = Ring(remote, z, z_plus, z_minus)
    ring_cot = Ring(remote, y, y_plus, y_minus)
    ring_a = [Ring(remote, x, x_plus, x_minus) for _ in range(PIECES)]
    ring_b = Ring(remote, x, x_plus, x_minus)
    ring_wg = Ring(remote, z, z_plus, z_minus)
    ring_cg = Ring(remote, x, x_plus, x_minus)
    ring_out = [Ring(remote, y, y_plus, y_minus) for _ in range(PIECES)]

    for h in (0, 1):
        ring_w.gather_first(w_block, h, w_hbm.at[pl.ds(h * S, S)])
    downs = []
    for h in (0, 1):
        half = pl.ds(h * (S // 2), S // 2)
        downs.append(
            move(cot_hbm.at[half], cot_relay.at[h], cot_relay.at[h], down, stays_down, local_sems.at[h])
        )

    load_a = pltpu.make_async_copy(qkv_a_hbm, qkv_a, local_sems.at[2])
    load_b = pltpu.make_async_copy(qkv_b_hbm, qkv_b, local_sems.at[3])
    load_w = pltpu.make_async_copy(w_hbm, w_all.at[:, at(z, S)], local_sems.at[4])
    load_a.start()
    load_b.start()
    load_w.start()

    handed = []
    load_a.wait()
    for block in causal_blocks():
        def head_a(h, carry, block=block):
            attend(qkv_a, h, block, ctx_a)
            return carry
        lax.fori_loop(0, HEADS, head_a, 0, unroll=3)
        p = block[0]
        copy = remote(ctx_a.at[block[1]], ctx_a_all.at[a_rows(p, x)], other_pipe)
        copy.start()
        handed.append(copy)

    acrosses = []
    for h in (0, 1):
        downs[h].wait_recv()
        landing = cot_all.at[at(2 * x + h, S // 2), at(core, W)]
        acrosses.append(
            move(cot_relay.at[h], landing, landing, across, stays_across, local_sems.at[5 + h])
        )

    load_b.wait()
    for h in (0, 1):
        def head_b(i, carry, h=h):
            attend_t(qkv_b, h * (HEADS // 2) + i, ctx_b_all, probs_t, x)
            return carry
        lax.fori_loop(0, HEADS // 2, head_b, 0, unroll=True)
        ring_b.gather_first(ctx_b_block, h)
        ring_b.gather_second(ctx_b_block, h)

    def to_twin(ref):
        copy = remote(ref, ref, twin)
        copy.start()
        return copy

    twins = []
    for h in (0, 1):
        acrosses[h].wait_recv()
        ring_cot.gather_first(cot_block, h)
        ring_cot.gather_second(cot_block, h)
        twins.append(to_twin(cot_block(y, h)))
    ring_w.gather_forward(w_block)
    for h in (0, 1):
        ring_w.gather_second(w_block, h, w_hbm.at[pl.ds(h * S, S)])
    ring_b.gather_forward(ctx_b_block)
    for p in range(PIECES):
        handed[p].wait_recv()
        for h in (0, 1):
            ring_a[p].gather_first(ctx_a_block(p), h)
        for h in (0, 1):
            ring_a[p].gather_second(ctx_a_block(p), h)
    ring_cot.gather_forward(cot_block)
    ring_cot.gather_near()
    for i in (mod4(y - 1), mod4(y + 1)):
        twins.append(to_twin(cot_all.at[at(place_tokens(i), S), at(core, W)]))
    ring_b.gather_near()
    ring_b.gather_far()
    for p in range(PIECES):
        ring_a[p].gather_forward(ctx_a_block(p))
    ring_cot.gather_far()
    twins.append(to_twin(cot_all.at[at(place_tokens(y + 2), S), at(core, W)]))
    for copy in twins:
        copy.wait_recv()

    def w_term(i):
        def rows(r, carry):
            w_part[i, r] = jnp.dot(
                ctx_b_all[at(r, S), :], cot_all[:, at(i, S)], preferred_element_type=F32
            ).astype(BF)
            return carry
        lax.fori_loop(0, 2, rows, 0)

    w_term(mod4(z + 2))
    ring_wg.reduce_far(w_part_block, w_far)
    w_term(mod4(z + 1))
    w_term(mod4(z - 1))
    ring_wg.reduce_near(w_part_block, w_near)
    w_term(z)

    load_w.wait()
    ring_w.gather_near()
    ring_w.gather_far()

    def o_term(p, side):
        return jnp.dot(
            ctx_a_all[at(p, 4 * HEAD_DIM), :], w_all[:, at(side, W)], preferred_element_type=F32
        )

    swaps = []
    for p in range(PIECES):
        ring_a[p].gather_near()
        ring_a[p].gather_far()
        rows = at(p, 4 * HEAD_DIM)
        o_other[rows] = o_term(p, 1 - core).astype(BF)
        copy = remote(o_other.at[rows], o_got.at[rows], twin)
        copy.start()
        swaps.append(copy)

    for p in range(PIECES):
        rows = at(p, 4 * HEAD_DIM)
        term = o_term(p, core)
        swaps[p].wait_recv()
        o_own[rows] = (term + o_got[rows].astype(F32)).astype(BF)
        ring_out[p].reduce_far(o_block(p), o_far.at[p])
        ring_out[p].reduce_near(o_block(p), o_near.at[p])
        if p > 0:
            ring_out[p - 1].reduce_pass(o_block(p - 1), o_far.at[p - 1], o_near.at[p - 1])

    def c_term(i):
        def rows(r, carry):
            c_part[i, r] = lax.dot_general(
                cot_all[at(2 * i + r, S // 2), :], w_all[...], NT, preferred_element_type=F32
            ).astype(BF)
            return carry
        lax.fori_loop(0, 2, rows, 0)

    back = []

    def o_finish(p):
        rows = pl.ds(p * HEAD_DIM, HEAD_DIM)
        for h in (0, 1):
            o_done[rows, pl.ds(h * S, S)] = (
                ring_out[p].reduce_sum(o_block(p), o_near.at[p], h).astype(BF)
            )
        back.append(
            move(
                o_done.at[rows], out_ref.at[rows], out_ref.at[rows], home, stays_home, local_sems.at[7 + p]
            )
        )

    c_term(mod4(x + 2))
    ring_cg.reduce_far(c_part_block, c_far)
    ring_out[2].reduce_pass(o_block(2), o_far.at[2], o_near.at[2])
    c_term(mod4(x + 1))
    c_term(mod4(x - 1))
    ring_cg.reduce_near(c_part_block, c_near)
    c_term(x)
    ring_wg.reduce_pass(w_part_block, w_far, w_near)
    ring_cg.reduce_pass(c_part_block, c_far, c_near)
    o_finish(0)
    o_finish(1)
    o_finish(2)

    for h in (0, 1):
        c_grad[pl.ds(h * (S // 2), S // 2)] = ring_cg.reduce_sum(c_part_block, c_near, h).astype(BF)

    def head_grad(h, carry):
        attend_grad(qkv_b, h, probs_t, c_grad, grads_ref)
        return carry

    lax.fori_loop(0, HEADS, head_grad, 0, unroll=2)

    for h in (0, 1):
        w_grad_ref[pl.ds(h * S, S)] = (
            ring_wg.reduce_sum(w_part_block, w_near, h) / lax.axis_size("dp")
        ).astype(BF)

    for copy in back:
        copy.wait_recv()

    moved = [m.copy for m in moves]
    for copy in made:
        if not any(copy is other for other in moved):
            copy.wait_send()
    for m in moves:
        m.wait_send()


def body(sent_qkv, saved_qkv, cotangent, out_weight):
    bf = lambda *shape: pltpu.VMEM(shape, BF)
    half = S // 2
    out, grads, w_grad = pl.pallas_call(
        kernel,
        out_shape=(
            jax.ShapeDtypeStruct((S, W), BF),
            jax.ShapeDtypeStruct((3, S, W), BF),
            jax.ShapeDtypeStruct((W, S), BF),
        ),
        in_specs=[pl.BlockSpec(memory_space=pl.ANY)] * 4,
        out_specs=(pl.BlockSpec(memory_space=pltpu.VMEM),) * 3,
        scratch_shapes=[
            bf(3, S, W), bf(3, S, W),
            bf(W, 4 * S), bf(4 * S, 2 * W), bf(2, half, W),
            bf(S, W), bf(4 * S, W), bf(W, 4 * S),
            pltpu.VMEM((HEADS, S, S), F32),
            bf(4, 2, S, S), bf(2, S, S), bf(2, 2, S, S),
            bf(4, 2, half, W), bf(2, half, W), bf(2, 2, half, W), bf(S, W),
            bf(4 * S, W), bf(4 * S, W), bf(4 * S, W),
            bf(PIECES, 2, HEAD_DIM, S), bf(PIECES, 2, 2, HEAD_DIM, S), bf(S, W),
            pltpu.SemaphoreType.DMA((N_SEMS,)),
            pltpu.SemaphoreType.DMA((N_SEMS,)),
            pltpu.SemaphoreType.DMA((10,)),
        ],
        compiler_params=pltpu.CompilerParams(
            collective_id=0, has_side_effects=True, vmem_limit_bytes=56 << 20
        ),
        cost_estimate=pl.CostEstimate(
            flops=13_000_000_000, bytes_accessed=16_000_000, transcendentals=1_800_000
        ),
    )(
        jnp.transpose(sent_qkv[0, 0], (1, 0, 2)),
        jnp.transpose(saved_qkv[0, 0], (1, 0, 2)),
        cotangent[0, 0],
        out_weight[0],
    )
    return out[None, None], jnp.transpose(grads, (1, 0, 2))[None, None], w_grad[None]


def solution(mesh):
    in_specs = (
        P("pipe", "dp", None, None, "tensor"),
        P("pipe", "dp", None, None, "tensor"),
        P("pipe", "dp", None, "tensor"),
        P("pipe", "tensor", "dp"),
    )
    out_specs = (
        P("pipe", "dp", None, "tensor"),
        P("pipe", "dp", None, None, "tensor"),
        P("pipe", "tensor", "dp"),
    )
    return jax.shard_map(body, mesh=mesh, in_specs=in_specs, out_specs=out_specs, check_vma=False)
```

```python
import math

import jax
import jax.numpy as jnp
from jax import lax
from jax.experimental import pallas as pl
from jax.experimental.pallas import tpu as pltpu
from jax.sharding import PartitionSpec as P

HEAD_DIM = 128
SCALE = 1.0 / math.sqrt(HEAD_DIM)
MESH = pl.DeviceIdType.MESH
BF = jnp.bfloat16
F32 = jnp.float32
S = 384
W = 768
HEADS = W // HEAD_DIM
N_SEMS = 96
PIECES = S // HEAD_DIM

NT = (((1,), (1,)), ((), ()))
TN = (((0,), (0,)), ((), ()))


def at(index, size):
    return pl.ds(pl.multiple_of(index * size, size), size)


def mod4(i):
    return lax.rem(i + 4, 4)


def causal_blocks():
    for r in range(S // HEAD_DIM):
        yield r, pl.ds(r * HEAD_DIM, HEAD_DIM), pl.ds(0, (r + 1) * HEAD_DIM)


def probs_of_block(qkv, cols, r, mine, seen):
    scores = lax.dot_general(qkv[1, seen, cols], qkv[0, mine, cols], NT, preferred_element_type=F32)
    row = lax.broadcasted_iota(jnp.int32, scores.shape, 0)
    col = lax.broadcasted_iota(jnp.int32, scores.shape, 1) + r * HEAD_DIM
    scores = jnp.where(row <= col, scores, -jnp.inf)
    weights = jnp.exp((scores - jnp.max(scores, axis=0, keepdims=True)) * SCALE)
    return weights * (1.0 / jnp.sum(weights, axis=0, keepdims=True))


def attend(qkv, h, block, context):
    cols = at(h, HEAD_DIM)
    r, mine, seen = block
    probs = probs_of_block(qkv, cols, r, mine, seen).astype(BF)
    context_t = lax.dot_general(qkv[2, seen, cols], probs, TN, preferred_element_type=F32)
    context[mine, cols] = context_t.T.astype(BF)


def attend_t(qkv, h, context_t, probs_t, x):
    cols = at(h, HEAD_DIM)
    for r, mine, seen in causal_blocks():
        probs = probs_of_block(qkv, cols, r, mine, seen)
        probs_t[h, seen, mine] = probs
        context_t[cols, at(x * (S // HEAD_DIM) + r, HEAD_DIM)] = lax.dot_general(
            qkv[2, seen, cols], probs.astype(BF), TN, preferred_element_type=F32
        ).astype(BF)


def attend_grad(qkv, h, probs_t, upstream, grads):
    cols = at(h, HEAD_DIM)
    dk, dv = [0.0] * 3, [0.0] * 3
    for r, mine, seen in causal_blocks():
        probs = probs_t[h, seen, mine]
        up = upstream[mine, cols]
        d_probs = lax.dot_general(qkv[2, seen, cols], up, NT, preferred_element_type=F32)
        total = jnp.sum(probs * d_probs, axis=0, keepdims=True)
        d_scores = (probs * (d_probs - total) * SCALE).astype(BF)
        dq_t = lax.dot_general(qkv[1, seen, cols], d_scores, TN, preferred_element_type=F32)
        grads[0, mine, cols] = dq_t.T.astype(BF)
        dk_r = jnp.dot(d_scores, qkv[0, mine, cols], preferred_element_type=F32)
        dv_r = jnp.dot(probs.astype(BF), up, preferred_element_type=F32)
        for j in range(r + 1):
            rows = slice(j * HEAD_DIM, (j + 1) * HEAD_DIM)
            dk[j] += dk_r[rows]
            dv[j] += dv_r[rows]
    for j in range(3):
        rows = pl.ds(j * HEAD_DIM, HEAD_DIM)
        grads[1, rows, cols] = dk[j].astype(BF)
        grads[2, rows, cols] = dv[j].astype(BF)


class Ring:
    def __init__(self, remote, me, plus, minus):
        self.remote, self.me, self.plus, self.minus = remote, me, plus, minus

    def gather_first(self, block, h, source=None):
        dst = block(self.me, h)
        copy = self.remote(dst if source is None else source, dst, (self.plus, self.minus)[h])
        copy.start()
        if h == 0:
            self.plus0 = copy
        else:
            self.minus1 = copy

    def gather_second(self, block, h, source=None):
        dst = block(self.me, h)
        copy = self.remote(dst if source is None else source, dst, (self.minus, self.plus)[h])
        copy.start()
        if h == 0:
            self.minus0 = copy
        else:
            self.plus1 = copy

    def gather_forward(self, block):
        prev, nxt = mod4(self.me - 1), mod4(self.me + 1)
        self.plus0.wait_recv()
        self.far0 = self.remote(block(prev, 0), block(prev, 0), self.plus)
        self.far0.start()
        self.minus1.wait_recv()
        self.far1 = self.remote(block(nxt, 1), block(nxt, 1), self.minus)
        self.far1.start()

    def gather_near(self):
        self.plus1.wait_recv()
        self.minus0.wait_recv()

    def gather_far(self):
        self.far0.wait_recv()
        self.far1.wait_recv()

    def reduce_far(self, part, got_far):
        far = mod4(self.me + 2)
        self.r0 = self.remote(part(far, 0), got_far.at[0], self.plus)
        self.r1 = self.remote(part(far, 1), got_far.at[1], self.minus)
        self.r0.start()
        self.r1.start()

    def reduce_near(self, part, got_near):
        nxt, prev = mod4(self.me + 1), mod4(self.me - 1)
        self.r2 = self.remote(part(nxt, 1), got_near.at[0, 1], self.plus)
        self.r3 = self.remote(part(prev, 0), got_near.at[1, 0], self.minus)
        self.r2.start()
        self.r3.start()

    def reduce_pass(self, part, got_far, got_near):
        nxt, prev = mod4(self.me + 1), mod4(self.me - 1)
        self.r0.wait_recv()
        ref = part(nxt, 0)
        ref[...] = (ref[...].astype(F32) + got_far[0].astype(F32)).astype(BF)
        self.r4 = self.remote(ref, got_near.at[0, 0], self.plus)
        self.r4.start()
        self.r1.wait_recv()
        ref = part(prev, 1)
        ref[...] = (ref[...].astype(F32) + got_far[1].astype(F32)).astype(BF)
        self.r5 = self.remote(ref, got_near.at[1, 1], self.minus)
        self.r5.start()

    def reduce_sum(self, part, got_near, h):
        for copy in ((self.r4, self.r3), (self.r2, self.r5))[h]:
            copy.wait_recv()
        total = part(self.me, h)[...].astype(F32)
        return total + got_near[0, h].astype(F32) + got_near[1, h].astype(F32)


def kernel(
    qkv_a_hbm, qkv_b_hbm, cot_hbm, w_hbm,
    out_ref, grads_ref, w_grad_ref,
    qkv_a, qkv_b, w_all, cot_all, cot_relay, ctx_a, ctx_a_all, ctx_b_all, probs_t,
    w_part, w_far, w_near, c_part, c_far, c_near, c_grad,
    o_own, o_other, o_got, o_far, o_near, o_done,
    send_sems, recv_sems, local_sems,
):
    dp, pipe, tensor = lax.axis_index("dp"), lax.axis_index("pipe"), lax.axis_index("tensor")
    x, z, y, core = dp // 4, lax.rem(dp, 4), tensor // 2, lax.rem(tensor, 2)

    def device(x=x, z=z, pipe=pipe, y=y, core=core):
        return (x * 4 + z, pipe, y * 2 + core)

    x_plus, x_minus = device(x=mod4(x + 1)), device(x=mod4(x - 1))
    y_plus, y_minus = device(y=mod4(y + 1)), device(y=mod4(y - 1))
    z_plus, z_minus = device(z=mod4(z + 1)), device(z=mod4(z - 1))
    twin, other_pipe = device(core=1 - core), device(pipe=1 - pipe)

    there = mod4(y - x + 2 * core)
    down, across = device(y=mod4(x + y + 2 * core)), device(x=there)
    home, away = device(x=there, y=x), device(x=y, y=mod4(x + y + 2 * core))
    stays_down, stays_across = lax.rem(x + 2 * core, 4) == 0, there == x
    stays_home = jnp.logical_and(there == x, y == x)

    barrier = pltpu.get_barrier_semaphore()
    for partner in (
        x_plus, x_minus, device(x=mod4(x + 2)), y_plus, y_minus, device(y=mod4(y + 2)),
        z_plus, z_minus, twin, other_pipe,
    ):
        pl.semaphore_signal(barrier, inc=1, device_id=partner, device_id_type=MESH)

    @pl.when(jnp.logical_not(stays_home))
    def _():
        for partner in (home, away):
            pl.semaphore_signal(barrier, inc=1, device_id=partner, device_id_type=MESH)

    pl.semaphore_wait(barrier, jnp.where(stays_home, 10, 12))

    made = []

    def remote(src, dst, where):
        copy = pltpu.make_async_remote_copy(
            src_ref=src, dst_ref=dst,
            send_sem=send_sems.at[len(made)], recv_sem=recv_sems.at[len(made)],
            device_id=where, device_id_type=MESH,
        )
        made.append(copy)
        return copy

    class Move:
        def __init__(self, src, dst_there, dst_here, where, stays, local_sem):
            self.stays, self.copy = stays, remote(src, dst_there, where)
            self.local = pltpu.make_async_copy(src, dst_here, local_sem)

        def start(self):
            pl.when(self.stays)(lambda: self.local.start())
            pl.when(jnp.logical_not(self.stays))(lambda: self.copy.start())

        def wait_recv(self):
            pl.when(self.stays)(lambda: self.local.wait())
            pl.when(jnp.logical_not(self.stays))(lambda: self.copy.wait_recv())

        def wait_send(self):
            pl.when(jnp.logical_not(self.stays))(lambda: self.copy.wait_send())

    moves = []

    def move(*args):
        moves.append(Move(*args))
        moves[-1].start()
        return moves[-1]

    def place_tokens(i):
        return mod4(i - x + 2 * core)

    def w_block(i, h):
        return w_all.at[pl.ds(h * S, S), at(i, S)]

    def cot_block(i, h):
        return cot_all.at[at(2 * place_tokens(i) + h, S // 2), at(core, W)]

    def a_rows(p, i):
        return at(p * 4 + i, HEAD_DIM)

    def ctx_a_block(p):
        return lambda i, h: ctx_a_all.at[a_rows(p, i), pl.ds(h * S, S)]

    def ctx_b_block(i, h):
        return ctx_b_all.at[pl.ds(h * S, S), at(i, S)]

    def w_part_block(i, h):
        return w_part.at[i, h]

    def c_part_block(i, h):
        return c_part.at[i, h]

    def o_block(p):
        return lambda i, h: o_own.at[a_rows(p, place_tokens(i)), pl.ds(h * S, S)]

    ring_w = Ring(remote, z, z_plus, z_minus)
    ring_cot = Ring(remote, y, y_plus, y_minus)
    ring_a = [Ring(remote, x, x_plus, x_minus) for _ in range(PIECES)]
    ring_b = Ring(remote, x, x_plus, x_minus)
    ring_wg = Ring(remote, z, z_plus, z_minus)
    ring_cg = Ring(remote, x, x_plus, x_minus)
    ring_out = [Ring(remote, y, y_plus, y_minus) for _ in range(PIECES)]

    for h in (0, 1):
        ring_w.gather_first(w_block, h, w_hbm.at[pl.ds(h * S, S)])
    downs = []
    for h in (0, 1):
        half = pl.ds(h * (S // 2), S // 2)
        downs.append(
            move(cot_hbm.at[half], cot_relay.at[h], cot_relay.at[h], down, stays_down, local_sems.at[h])
        )

    load_a = pltpu.make_async_copy(qkv_a_hbm, qkv_a, local_sems.at[2])
    load_b = pltpu.make_async_copy(qkv_b_hbm, qkv_b, local_sems.at[3])
    load_w = pltpu.make_async_copy(w_hbm, w_all.at[:, at(z, S)], local_sems.at[4])
    load_a.start()
    load_b.start()
    load_w.start()

    handed = []
    load_a.wait()
    for block in causal_blocks():
        def head_a(h, carry, block=block):
            attend(qkv_a, h, block, ctx_a)
            return carry
        lax.fori_loop(0, HEADS, head_a, 0, unroll=3)
        p = block[0]
        copy = remote(ctx_a.at[block[1]], ctx_a_all.at[a_rows(p, x)], other_pipe)
        copy.start()
        handed.append(copy)

    acrosses = []
    for h in (0, 1):
        downs[h].wait_recv()
        landing = cot_all.at[at(2 * x + h, S // 2), at(core, W)]
        acrosses.append(
            move(cot_relay.at[h], landing, landing, across, stays_across, local_sems.at[5 + h])
        )

    load_b.wait()
    for h in (0, 1):
        def head_b(i, carry, h=h):
            attend_t(qkv_b, h * (HEADS // 2) + i, ctx_b_all, probs_t, x)
            return carry
        lax.fori_loop(0, HEADS // 2, head_b, 0, unroll=True)
        ring_b.gather_first(ctx_b_block, h)
        ring_b.gather_second(ctx_b_block, h)

    def to_twin(ref):
        copy = remote(ref, ref, twin)
        copy.start()
        return copy

    twins = []
    for h in (0, 1):
        acrosses[h].wait_recv()
        ring_cot.gather_first(cot_block, h)
        ring_cot.gather_second(cot_block, h)
        twins.append(to_twin(cot_block(y, h)))
    ring_w.gather_forward(w_block)
    for h in (0, 1):
        ring_w.gather_second(w_block, h, w_hbm.at[pl.ds(h * S, S)])
    ring_b.gather_forward(ctx_b_block)
    for p in range(PIECES):
        handed[p].wait_recv()
        for h in (0, 1):
            ring_a[p].gather_first(ctx_a_block(p), h)
        for h in (0, 1):
            ring_a[p].gather_second(ctx_a_block(p), h)
    ring_cot.gather_forward(cot_block)
    ring_cot.gather_near()
    for i in (mod4(y - 1), mod4(y + 1)):
        twins.append(to_twin(cot_all.at[at(place_tokens(i), S), at(core, W)]))
    ring_b.gather_near()
    ring_b.gather_far()
    for p in range(PIECES):
        ring_a[p].gather_forward(ctx_a_block(p))
    ring_cot.gather_far()
    twins.append(to_twin(cot_all.at[at(place_tokens(y + 2), S), at(core, W)]))
    for copy in twins:
        copy.wait_recv()

    def w_terms(pair):
        def rows(r, carry):
            term = jnp.dot(
                ctx_b_all[at(r, S), :], cot_all[:, at(pair, W)], preferred_element_type=F32
            ).astype(BF)
            w_part[2 * pair, r], w_part[2 * pair + 1, r] = term[:, :S], term[:, S:]
            return carry
        lax.fori_loop(0, 2, rows, 0)

    w_terms(1 - z // 2)
    ring_wg.reduce_far(w_part_block, w_far)
    w_terms(z // 2)
    ring_wg.reduce_near(w_part_block, w_near)

    load_w.wait()
    ring_w.gather_near()
    ring_w.gather_far()

    def o_term(p, side):
        return jnp.dot(
            ctx_a_all[at(p, 4 * HEAD_DIM), :], w_all[:, at(side, W)], preferred_element_type=F32
        )

    def c_term(i):
        term = lax.dot_general(
            cot_all[at(i, S), :], w_all[...], NT, preferred_element_type=F32
        ).astype(BF)
        c_part[i, 0], c_part[i, 1] = term[: S // 2], term[S // 2 :]

    back = []

    def o_finish(p):
        rows = pl.ds(p * HEAD_DIM, HEAD_DIM)
        for h in (0, 1):
            o_done[rows, pl.ds(h * S, S)] = (
                ring_out[p].reduce_sum(o_block(p), o_near.at[p], h).astype(BF)
            )
        back.append(
            move(
                o_done.at[rows], out_ref.at[rows], out_ref.at[rows], home, stays_home, local_sems.at[7 + p]
            )
        )

    c_term(mod4(x + 2))
    ring_cg.reduce_far(c_part_block, c_far)
    swaps = []
    for p in range(PIECES):
        ring_a[p].gather_near()
        ring_a[p].gather_far()
        rows = at(p, 4 * HEAD_DIM)
        o_other[rows] = o_term(p, 1 - core).astype(BF)
        copy = remote(o_other.at[rows], o_got.at[rows], twin)
        copy.start()
        swaps.append(copy)

    for p in range(PIECES):
        rows = at(p, 4 * HEAD_DIM)
        term = o_term(p, core)
        swaps[p].wait_recv()
        o_own[rows] = (term + o_got[rows].astype(F32)).astype(BF)
        ring_out[p].reduce_far(o_block(p), o_far.at[p])
        ring_out[p].reduce_near(o_block(p), o_near.at[p])

    c_term(mod4(x + 1))
    c_term(mod4(x - 1))
    ring_cg.reduce_near(c_part_block, c_near)
    for p in range(PIECES):
        ring_out[p].reduce_pass(o_block(p), o_far.at[p], o_near.at[p])
    c_term(x)
    ring_cg.reduce_pass(c_part_block, c_far, c_near)
    ring_wg.reduce_pass(w_part_block, w_far, w_near)
    o_finish(0)
    o_finish(1)
    o_finish(2)

    for h in (0, 1):
        c_grad[pl.ds(h * (S // 2), S // 2)] = ring_cg.reduce_sum(c_part_block, c_near, h).astype(BF)

    def head_grad(h, carry):
        attend_grad(qkv_b, h, probs_t, c_grad, grads_ref)
        return carry

    lax.fori_loop(0, HEADS, head_grad, 0, unroll=2)

    for h in (0, 1):
        w_grad_ref[pl.ds(h * S, S)] = (
            ring_wg.reduce_sum(w_part_block, w_near, h) / lax.axis_size("dp")
        ).astype(BF)

    for copy in back:
        copy.wait_recv()

    moved = [m.copy for m in moves]
    for copy in made:
        if not any(copy is other for other in moved):
            copy.wait_send()
    for m in moves:
        m.wait_send()


def body(sent_qkv, saved_qkv, cotangent, out_weight):
    bf = lambda *shape: pltpu.VMEM(shape, BF)
    half = S // 2
    out, grads, w_grad = pl.pallas_call(
        kernel,
        out_shape=(
            jax.ShapeDtypeStruct((S, W), BF),
            jax.ShapeDtypeStruct((3, S, W), BF),
            jax.ShapeDtypeStruct((W, S), BF),
        ),
        in_specs=[pl.BlockSpec(memory_space=pl.ANY)] * 4,
        out_specs=(pl.BlockSpec(memory_space=pltpu.VMEM),) * 3,
        scratch_shapes=[
            bf(3, S, W), bf(3, S, W),
            bf(W, 4 * S), bf(4 * S, 2 * W), bf(2, half, W),
            bf(S, W), bf(4 * S, W), bf(W, 4 * S),
            pltpu.VMEM((HEADS, S, S), F32),
            bf(4, 2, S, S), bf(2, S, S), bf(2, 2, S, S),
            bf(4, 2, half, W), bf(2, half, W), bf(2, 2, half, W), bf(S, W),
            bf(4 * S, W), bf(4 * S, W), bf(4 * S, W),
            bf(PIECES, 2, HEAD_DIM, S), bf(PIECES, 2, 2, HEAD_DIM, S), bf(S, W),
            pltpu.SemaphoreType.DMA((N_SEMS,)),
            pltpu.SemaphoreType.DMA((N_SEMS,)),
            pltpu.SemaphoreType.DMA((10,)),
        ],
        compiler_params=pltpu.CompilerParams(
            collective_id=0, has_side_effects=True, vmem_limit_bytes=56 << 20
        ),
        cost_estimate=pl.CostEstimate(
            flops=13_000_000_000, bytes_accessed=16_000_000, transcendentals=1_800_000
        ),
    )(
        jnp.transpose(sent_qkv[0, 0], (1, 0, 2)),
        jnp.transpose(saved_qkv[0, 0], (1, 0, 2)),
        cotangent[0, 0],
        out_weight[0],
    )
    return out[None, None], jnp.transpose(grads, (1, 0, 2))[None, None], w_grad[None]


def solution(mesh):
    in_specs = (
        P("pipe", "dp", None, None, "tensor"),
        P("pipe", "dp", None, None, "tensor"),
        P("pipe", "dp", None, "tensor"),
        P("pipe", "tensor", "dp"),
    )
    out_specs = (
        P("pipe", "dp", None, "tensor"),
        P("pipe", "dp", None, None, "tensor"),
        P("pipe", "tensor", "dp"),
    )
    return jax.shard_map(body, mesh=mesh, in_specs=in_specs, out_specs=out_specs, check_vma=False)
```

```python
import math

import jax
import jax.numpy as jnp
from jax import lax
from jax.experimental import pallas as pl
from jax.experimental.pallas import tpu as pltpu
from jax.sharding import PartitionSpec as P

HEAD_DIM = 128
SCALE = 1.0 / math.sqrt(HEAD_DIM)
MESH = pl.DeviceIdType.MESH
BF = jnp.bfloat16
F32 = jnp.float32
S = 384
W = 768
HEADS = W // HEAD_DIM
N_SEMS = 96
PIECES = S // HEAD_DIM

NT = (((1,), (1,)), ((), ()))
TN = (((0,), (0,)), ((), ()))


def at(index, size):
    return pl.ds(pl.multiple_of(index * size, size), size)


def mod4(i):
    return lax.rem(i + 4, 4)


def causal_blocks():
    for r in range(S // HEAD_DIM):
        yield r, pl.ds(r * HEAD_DIM, HEAD_DIM), pl.ds(0, (r + 1) * HEAD_DIM)


def probs_of_block(qkv, cols, r, mine, seen):
    scores = lax.dot_general(qkv[1, seen, cols], qkv[0, mine, cols], NT, preferred_element_type=F32)
    row = lax.broadcasted_iota(jnp.int32, scores.shape, 0)
    col = lax.broadcasted_iota(jnp.int32, scores.shape, 1) + r * HEAD_DIM
    scores = jnp.where(row <= col, scores, -jnp.inf)
    weights = jnp.exp((scores - jnp.max(scores, axis=0, keepdims=True)) * SCALE)
    return weights * (1.0 / jnp.sum(weights, axis=0, keepdims=True))


def attend(qkv, h, block, context):
    cols = at(h, HEAD_DIM)
    r, mine, seen = block
    probs = probs_of_block(qkv, cols, r, mine, seen).astype(BF)
    context_t = lax.dot_general(qkv[2, seen, cols], probs, TN, preferred_element_type=F32)
    context[mine, cols] = context_t.T.astype(BF)


def attend_t(qkv, h, context_t, probs_t, x):
    cols = at(h, HEAD_DIM)
    for r, mine, seen in causal_blocks():
        probs = probs_of_block(qkv, cols, r, mine, seen)
        probs_t[h, seen, mine] = probs
        context_t[cols, at(x * (S // HEAD_DIM) + r, HEAD_DIM)] = lax.dot_general(
            qkv[2, seen, cols], probs.astype(BF), TN, preferred_element_type=F32
        ).astype(BF)


def attend_grad(qkv, h, probs_t, upstream, grads):
    cols = at(h, HEAD_DIM)
    dk, dv = [0.0] * 3, [0.0] * 3
    for r, mine, seen in causal_blocks():
        probs = probs_t[h, seen, mine]
        up = upstream[mine, cols]
        d_probs = lax.dot_general(qkv[2, seen, cols], up, NT, preferred_element_type=F32)
        total = jnp.sum(probs * d_probs, axis=0, keepdims=True)
        d_scores = (probs * (d_probs - total) * SCALE).astype(BF)
        dq_t = lax.dot_general(qkv[1, seen, cols], d_scores, TN, preferred_element_type=F32)
        grads[0, mine, cols] = dq_t.T.astype(BF)
        dk_r = jnp.dot(d_scores, qkv[0, mine, cols], preferred_element_type=F32)
        dv_r = jnp.dot(probs.astype(BF), up, preferred_element_type=F32)
        for j in range(r + 1):
            rows = slice(j * HEAD_DIM, (j + 1) * HEAD_DIM)
            dk[j] += dk_r[rows]
            dv[j] += dv_r[rows]
    for j in range(3):
        rows = pl.ds(j * HEAD_DIM, HEAD_DIM)
        grads[1, rows, cols] = dk[j].astype(BF)
        grads[2, rows, cols] = dv[j].astype(BF)


class Ring:
    def __init__(self, remote, me, plus, minus):
        self.remote, self.me, self.plus, self.minus = remote, me, plus, minus

    def gather_first(self, block, h, source=None):
        dst = block(self.me, h)
        copy = self.remote(dst if source is None else source, dst, (self.plus, self.minus)[h])
        copy.start()
        if h == 0:
            self.plus0 = copy
        else:
            self.minus1 = copy

    def gather_second(self, block, h, source=None):
        dst = block(self.me, h)
        copy = self.remote(dst if source is None else source, dst, (self.minus, self.plus)[h])
        copy.start()
        if h == 0:
            self.minus0 = copy
        else:
            self.plus1 = copy

    def gather_forward(self, block):
        prev, nxt = mod4(self.me - 1), mod4(self.me + 1)
        self.plus0.wait_recv()
        self.far0 = self.remote(block(prev, 0), block(prev, 0), self.plus)
        self.far0.start()
        self.minus1.wait_recv()
        self.far1 = self.remote(block(nxt, 1), block(nxt, 1), self.minus)
        self.far1.start()

    def gather_near(self):
        self.plus1.wait_recv()
        self.minus0.wait_recv()

    def gather_far(self):
        self.far0.wait_recv()
        self.far1.wait_recv()

    def reduce_far(self, part, got_far):
        far = mod4(self.me + 2)
        self.r0 = self.remote(part(far, 0), got_far.at[0], self.plus)
        self.r1 = self.remote(part(far, 1), got_far.at[1], self.minus)
        self.r0.start()
        self.r1.start()

    def reduce_near(self, part, got_near):
        nxt, prev = mod4(self.me + 1), mod4(self.me - 1)
        self.r2 = self.remote(part(nxt, 1), got_near.at[0, 1], self.plus)
        self.r3 = self.remote(part(prev, 0), got_near.at[1, 0], self.minus)
        self.r2.start()
        self.r3.start()

    def reduce_pass(self, part, got_far, got_near):
        nxt, prev = mod4(self.me + 1), mod4(self.me - 1)
        self.r0.wait_recv()
        ref = part(nxt, 0)
        ref[...] = (ref[...].astype(F32) + got_far[0].astype(F32)).astype(BF)
        self.r4 = self.remote(ref, got_near.at[0, 0], self.plus)
        self.r4.start()
        self.r1.wait_recv()
        ref = part(prev, 1)
        ref[...] = (ref[...].astype(F32) + got_far[1].astype(F32)).astype(BF)
        self.r5 = self.remote(ref, got_near.at[1, 1], self.minus)
        self.r5.start()

    def reduce_sum(self, part, got_near, h):
        for copy in ((self.r4, self.r3), (self.r2, self.r5))[h]:
            copy.wait_recv()
        total = part(self.me, h)[...].astype(F32)
        return total + got_near[0, h].astype(F32) + got_near[1, h].astype(F32)


def kernel(
    qkv_a_hbm, qkv_b_hbm, cot_hbm, w_hbm,
    out_ref, grads_ref, w_grad_ref,
    qkv_a, qkv_b, w_all, cot_all, cot_relay, ctx_a, ctx_a_all, ctx_b_all, probs_t,
    w_part, w_far, w_near, c_part, c_far, c_near, c_grad,
    o_own, o_other, o_got, o_far, o_near, o_done, grads_v, w_grad_v,
    send_sems, recv_sems, local_sems,
):
    dp, pipe, tensor = lax.axis_index("dp"), lax.axis_index("pipe"), lax.axis_index("tensor")
    x, z, y, core = dp // 4, lax.rem(dp, 4), tensor // 2, lax.rem(tensor, 2)

    def device(x=x, z=z, pipe=pipe, y=y, core=core):
        return (x * 4 + z, pipe, y * 2 + core)

    x_plus, x_minus = device(x=mod4(x + 1)), device(x=mod4(x - 1))
    y_plus, y_minus = device(y=mod4(y + 1)), device(y=mod4(y - 1))
    z_plus, z_minus = device(z=mod4(z + 1)), device(z=mod4(z - 1))
    twin, other_pipe = device(core=1 - core), device(pipe=1 - pipe)

    there = mod4(y - x + 2 * core)
    down, across = device(y=mod4(x + y + 2 * core)), device(x=there)
    home, away = device(x=there, y=x), device(x=y, y=mod4(x + y + 2 * core))
    stays_down, stays_across = lax.rem(x + 2 * core, 4) == 0, there == x
    stays_home = jnp.logical_and(there == x, y == x)

    barrier = pltpu.get_barrier_semaphore()
    for partner in (
        x_plus, x_minus, device(x=mod4(x + 2)), y_plus, y_minus, device(y=mod4(y + 2)),
        z_plus, z_minus, twin, other_pipe,
    ):
        pl.semaphore_signal(barrier, inc=1, device_id=partner, device_id_type=MESH)

    @pl.when(jnp.logical_not(stays_home))
    def _():
        for partner in (home, away):
            pl.semaphore_signal(barrier, inc=1, device_id=partner, device_id_type=MESH)

    pl.semaphore_wait(barrier, jnp.where(stays_home, 10, 12))

    made = []

    def remote(src, dst, where):
        copy = pltpu.make_async_remote_copy(
            src_ref=src, dst_ref=dst,
            send_sem=send_sems.at[len(made)], recv_sem=recv_sems.at[len(made)],
            device_id=where, device_id_type=MESH,
        )
        made.append(copy)
        return copy

    class Move:
        def __init__(self, src, dst_there, dst_here, where, stays, local_sem):
            self.stays, self.copy = stays, remote(src, dst_there, where)
            self.local = pltpu.make_async_copy(src, dst_here, local_sem)

        def start(self):
            pl.when(self.stays)(lambda: self.local.start())
            pl.when(jnp.logical_not(self.stays))(lambda: self.copy.start())

        def wait_recv(self):
            pl.when(self.stays)(lambda: self.local.wait())
            pl.when(jnp.logical_not(self.stays))(lambda: self.copy.wait_recv())

        def wait_send(self):
            pl.when(jnp.logical_not(self.stays))(lambda: self.copy.wait_send())

    moves = []

    def move(*args):
        moves.append(Move(*args))
        moves[-1].start()
        return moves[-1]

    def place_tokens(i):
        return mod4(i - x + 2 * core)

    def w_block(i, h):
        return w_all.at[pl.ds(h * S, S), at(i, S)]

    def cot_block(i, h):
        return cot_all.at[at(2 * place_tokens(i) + h, S // 2), at(core, W)]

    def a_rows(p, i):
        return at(p * 4 + i, HEAD_DIM)

    def ctx_a_block(p):
        return lambda i, h: ctx_a_all.at[a_rows(p, i), pl.ds(h * S, S)]

    def ctx_b_block(i, h):
        return ctx_b_all.at[pl.ds(h * S, S), at(i, S)]

    def w_part_block(i, h):
        return w_part.at[i, h]

    def c_part_block(i, h):
        return c_part.at[i, h]

    def o_block(p):
        return lambda i, h: o_own.at[a_rows(p, place_tokens(i)), pl.ds(h * S, S)]

    ring_w = Ring(remote, z, z_plus, z_minus)
    ring_cot = Ring(remote, y, y_plus, y_minus)
    ring_a = [Ring(remote, x, x_plus, x_minus) for _ in range(PIECES)]
    ring_b = Ring(remote, x, x_plus, x_minus)
    ring_wg = Ring(remote, z, z_plus, z_minus)
    ring_cg = Ring(remote, x, x_plus, x_minus)
    ring_out = [Ring(remote, y, y_plus, y_minus) for _ in range(PIECES)]

    for h in (0, 1):
        ring_w.gather_first(w_block, h, w_hbm.at[pl.ds(h * S, S)])
    downs = []
    for h in (0, 1):
        half = pl.ds(h * (S // 2), S // 2)
        downs.append(
            move(cot_hbm.at[half], cot_relay.at[h], cot_relay.at[h], down, stays_down, local_sems.at[h])
        )

    load_a = pltpu.make_async_copy(qkv_a_hbm, qkv_a, local_sems.at[2])
    load_b = pltpu.make_async_copy(qkv_b_hbm, qkv_b, local_sems.at[3])
    load_w = pltpu.make_async_copy(w_hbm, w_all.at[:, at(z, S)], local_sems.at[4])
    load_a.start()
    load_b.start()
    load_w.start()

    handed = []
    load_a.wait()
    for block in causal_blocks():
        def head_a(h, carry, block=block):
            attend(qkv_a, h, block, ctx_a)
            return carry
        lax.fori_loop(0, HEADS, head_a, 0, unroll=3)
        p = block[0]
        copy = remote(ctx_a.at[block[1]], ctx_a_all.at[a_rows(p, x)], other_pipe)
        copy.start()
        handed.append(copy)

    acrosses = []
    for h in (0, 1):
        downs[h].wait_recv()
        landing = cot_all.at[at(2 * x + h, S // 2), at(core, W)]
        acrosses.append(
            move(cot_relay.at[h], landing, landing, across, stays_across, local_sems.at[5 + h])
        )

    load_b.wait()
    for h in (0, 1):
        def head_b(i, carry, h=h):
            attend_t(qkv_b, h * (HEADS // 2) + i, ctx_b_all, probs_t, x)
            return carry
        lax.fori_loop(0, HEADS // 2, head_b, 0, unroll=True)
        ring_b.gather_first(ctx_b_block, h)
        ring_b.gather_second(ctx_b_block, h)

    def to_twin(ref):
        copy = remote(ref, ref, twin)
        copy.start()
        return copy

    twins = []
    for h in (0, 1):
        acrosses[h].wait_recv()
        ring_cot.gather_first(cot_block, h)
        ring_cot.gather_second(cot_block, h)
        twins.append(to_twin(cot_block(y, h)))
    ring_w.gather_forward(w_block)
    for h in (0, 1):
        ring_w.gather_second(w_block, h, w_hbm.at[pl.ds(h * S, S)])
    ring_b.gather_forward(ctx_b_block)
    for p in range(PIECES):
        handed[p].wait_recv()
        for h in (0, 1):
            ring_a[p].gather_first(ctx_a_block(p), h)
        for h in (0, 1):
            ring_a[p].gather_second(ctx_a_block(p), h)
    ring_cot.gather_forward(cot_block)
    ring_cot.gather_near()
    for i in (mod4(y - 1), mod4(y + 1)):
        twins.append(to_twin(cot_all.at[at(place_tokens(i), S), at(core, W)]))
    ring_b.gather_near()
    ring_b.gather_far()
    for p in range(PIECES):
        ring_a[p].gather_forward(ctx_a_block(p))
    ring_cot.gather_far()
    twins.append(to_twin(cot_all.at[at(place_tokens(y + 2), S), at(core, W)]))
    for copy in twins:
        copy.wait_recv()

    def w_terms(pair):
        def rows(r, carry):
            term = jnp.dot(
                ctx_b_all[at(r, S), :], cot_all[:, at(pair, W)], preferred_element_type=F32
            ).astype(BF)
            w_part[2 * pair, r], w_part[2 * pair + 1, r] = term[:, :S], term[:, S:]
            return carry
        lax.fori_loop(0, 2, rows, 0)

    w_terms(1 - z // 2)
    ring_wg.reduce_far(w_part_block, w_far)
    w_terms(z // 2)
    ring_wg.reduce_near(w_part_block, w_near)

    load_w.wait()
    ring_w.gather_near()
    ring_w.gather_far()

    def o_term(p, side):
        return jnp.dot(
            ctx_a_all[at(p, 4 * HEAD_DIM), :], w_all[:, at(side, W)], preferred_element_type=F32
        )

    def c_term(i):
        term = lax.dot_general(
            cot_all[at(i, S), :], w_all[...], NT, preferred_element_type=F32
        ).astype(BF)
        c_part[i, 0], c_part[i, 1] = term[: S // 2], term[S // 2 :]

    back = []

    def o_finish(p):
        rows = pl.ds(p * HEAD_DIM, HEAD_DIM)
        for h in (0, 1):
            o_done[rows, pl.ds(h * S, S)] = (
                ring_out[p].reduce_sum(o_block(p), o_near.at[p], h).astype(BF)
            )
        back.append(
            move(
                o_done.at[rows], out_ref.at[rows], out_ref.at[rows], home, stays_home, local_sems.at[7 + p]
            )
        )

    c_term(mod4(x + 2))
    ring_cg.reduce_far(c_part_block, c_far)
    swaps = []
    for p in range(PIECES):
        ring_a[p].gather_near()
        ring_a[p].gather_far()
        rows = at(p, 4 * HEAD_DIM)
        o_other[rows] = o_term(p, 1 - core).astype(BF)
        copy = remote(o_other.at[rows], o_got.at[rows], twin)
        copy.start()
        swaps.append(copy)

    for p in range(PIECES):
        rows = at(p, 4 * HEAD_DIM)
        term = o_term(p, core)
        swaps[p].wait_recv()
        o_own[rows] = (term + o_got[rows].astype(F32)).astype(BF)
        ring_out[p].reduce_far(o_block(p), o_far.at[p])
        ring_out[p].reduce_near(o_block(p), o_near.at[p])

    c_term(mod4(x + 1))
    c_term(mod4(x - 1))
    ring_cg.reduce_near(c_part_block, c_near)
    for p in range(PIECES):
        ring_out[p].reduce_pass(o_block(p), o_far.at[p], o_near.at[p])
    c_term(x)
    ring_cg.reduce_pass(c_part_block, c_far, c_near)
    ring_wg.reduce_pass(w_part_block, w_far, w_near)
    o_finish(0)
    o_finish(1)
    o_finish(2)

    for h in (0, 1):
        c_grad[pl.ds(h * (S // 2), S // 2)] = ring_cg.reduce_sum(c_part_block, c_near, h).astype(BF)

    def head_grad(h, carry):
        attend_grad(qkv_b, h, probs_t, c_grad, grads_v)
        return carry

    lax.fori_loop(0, HEADS, head_grad, 0, unroll=2)
    stores = [pltpu.make_async_copy(grads_v, grads_ref, local_sems.at[10])]
    stores[0].start()

    for h in (0, 1):
        rows = pl.ds(h * S, S)
        w_grad_v[rows] = (
            ring_wg.reduce_sum(w_part_block, w_near, h) / lax.axis_size("dp")
        ).astype(BF)
        stores.append(
            pltpu.make_async_copy(w_grad_v.at[rows], w_grad_ref.at[rows], local_sems.at[11 + h])
        )
        stores[-1].start()

    for copy in back:
        copy.wait_recv()
    for copy in stores:
        copy.wait()

    moved = [m.copy for m in moves]
    for copy in made:
        if not any(copy is other for other in moved):
            copy.wait_send()
    for m in moves:
        m.wait_send()


def body(sent_qkv, saved_qkv, cotangent, out_weight):
    bf = lambda *shape: pltpu.VMEM(shape, BF)
    half = S // 2
    out, grads, w_grad = pl.pallas_call(
        kernel,
        out_shape=(
            jax.ShapeDtypeStruct((S, W), BF),
            jax.ShapeDtypeStruct((3, S, W), BF),
            jax.ShapeDtypeStruct((W, S), BF),
        ),
        in_specs=[pl.BlockSpec(memory_space=pl.ANY)] * 4,
        out_specs=(pl.BlockSpec(memory_space=pl.ANY),) * 3,
        scratch_shapes=[
            bf(3, S, W), bf(3, S, W),
            bf(W, 4 * S), bf(4 * S, 2 * W), bf(2, half, W),
            bf(S, W), bf(4 * S, W), bf(W, 4 * S),
            pltpu.VMEM((HEADS, S, S), F32),
            bf(4, 2, S, S), bf(2, S, S), bf(2, 2, S, S),
            bf(4, 2, half, W), bf(2, half, W), bf(2, 2, half, W), bf(S, W),
            bf(4 * S, W), bf(4 * S, W), bf(4 * S, W),
            bf(PIECES, 2, HEAD_DIM, S), bf(PIECES, 2, 2, HEAD_DIM, S), bf(S, W),
            bf(3, S, W), bf(W, S),
            pltpu.SemaphoreType.DMA((N_SEMS,)),
            pltpu.SemaphoreType.DMA((N_SEMS,)),
            pltpu.SemaphoreType.DMA((13,)),
        ],
        compiler_params=pltpu.CompilerParams(
            collective_id=0, has_side_effects=True, vmem_limit_bytes=56 << 20
        ),
        cost_estimate=pl.CostEstimate(
            flops=13_000_000_000, bytes_accessed=16_000_000, transcendentals=1_800_000
        ),
    )(
        jnp.transpose(sent_qkv[0, 0], (1, 0, 2)),
        jnp.transpose(saved_qkv[0, 0], (1, 0, 2)),
        cotangent[0, 0],
        out_weight[0],
    )
    return out[None, None], jnp.transpose(grads, (1, 0, 2))[None, None], w_grad[None]


def solution(mesh):
    in_specs = (
        P("pipe", "dp", None, None, "tensor"),
        P("pipe", "dp", None, None, "tensor"),
        P("pipe", "dp", None, "tensor"),
        P("pipe", "tensor", "dp"),
    )
    out_specs = (
        P("pipe", "dp", None, "tensor"),
        P("pipe", "dp", None, None, "tensor"),
        P("pipe", "tensor", "dp"),
    )
    return jax.shard_map(body, mesh=mesh, in_specs=in_specs, out_specs=out_specs, check_vma=False)
```
